256 devices in a mesh: dp: 16 (over z, x_hi), tensor: 16 (over y, x_lo, core).
Axes of the slice: x: 4 (x_hi: 2, x_lo: 2; x = x_hi * 2 + x_lo), y: 4, z: 8, core: 2. Of those that a mesh axis runs over, the one named last changes fastest.
Arguments:
- queries: bfloat16 [8192, 8192], P('dp', 'tensor'), may hold values from -20 to 20
- keys: bfloat16 [8192, 8192], P('dp', 'tensor'), may hold values from -20 to 20
- values: bfloat16 [8192, 8192], P('dp', 'tensor'), may hold values from -6 to 6
- out_grad: bfloat16 [8192, 8192], P('dp'), may hold values from -6 to 6
- o_weight: bfloat16 [8192, 8192], P('tensor', 'dp'), may hold values from -0.0625 to 0.0625
- exponents: int32 [8192], P('tensor'), may hold values from -2 to 2
- valid_lengths: int32 [16], P('dp'), may hold values from 128 to 512, as said below
Outputs:
- grad_queries: bfloat16 [8192, 8192], P('dp', 'tensor')
- grad_keys: bfloat16 [8192, 8192], P('dp', 'tensor')
- grad_values: bfloat16 [8192, 8192], P('dp', 'tensor')
- grad_weight: float32 [8192, 8192], P('tensor', 'dp')
The draws below stay inside these ranges and needn't reach their ends.
Inputs may be any that keep to these rules, and one draw needn't show every extreme that they name: `valid_lengths`: each block has at least 128 valid tokens; some block is full and some has exactly 128.
All inputs are finite; a program needn't handle non-finite values.
Results may differ from the reference program's by a relative error of at most 0.024.
Values may be sent and summed in bfloat16 or wider, within the bound.
No kernel may reach another device: no remote copies, remote signals or barrier semaphores. Data moves between devices by JAX's collectives and lax.ppermute only.
A program may use at most 128 MiB of HBM per device.

```python
import math
import jax
import jax.numpy as jnp
from jax import lax

HEADS = 64
HEAD_DIM = 128
D = 8192
TOK_DEV = 512
TOKENS = 8192
BLOCKS = 16


def draw_queries(key, part):
    key = jax.random.fold_in(key, 3)
    own = jax.random.truncated_normal(key, -4.0, 4.0, (TOKENS, D), jnp.float32)
    return own.astype(jnp.bfloat16)


def draw_keys(key, part):
    key = jax.random.fold_in(key, 5)
    own = jax.random.truncated_normal(key, -4.0, 4.0, (TOKENS, D), jnp.float32)
    return own.astype(jnp.bfloat16)


def draw_valid_lengths(key, part):
    key = jax.random.fold_in(key, 7)
    drawn = jax.random.randint(jax.random.fold_in(key, 1), (BLOCKS,), TOK_DEV // 4, TOK_DEV + 1, dtype=jnp.int32)
    order = jax.random.permutation(jax.random.fold_in(key, 2), BLOCKS)
    drawn = drawn.at[order[0]].set(TOK_DEV)
    drawn = drawn.at[order[1]].set(TOK_DEV // 4)
    return drawn


def with_ends(values, stream_key, least, high):
    extent = values.shape
    place = [jax.random.randint(jax.random.fold_in(stream_key, axis), (), 0, extent[axis]) for axis in range(len(extent))]
    values = values.at[tuple(place)].set(least)
    longest = extent.index(max(extent))
    place[longest] = (place[longest] + 1) % extent[longest]
    return values.at[tuple(place)].set(high)


def spiked(values, rng, source, target, shards_of, factor):
    owner, partner = [(jnp.arange(values.shape[axis_at]) // (values.shape[axis_at] // shards_of)).reshape([-1 if axis == axis_at else 1 for axis in range(values.ndim)]) for axis_at in (source, target)]
    chosen = jax.random.permutation(rng, shards_of)[partner]
    strong = (owner == chosen) | (owner == (partner + shards_of // 2) % shards_of)
    return jnp.where(strong, factor * values, values)


def shard_levels(rng, extent, cuts, least, top_value):
    gain, own = 1.0, jax.random.fold_in(rng, 6)
    for axis_at, parts in cuts:
        draws = jnp.exp(jax.random.uniform(jax.random.fold_in(own, axis_at), (parts,), jnp.float32, least / len(cuts), top_value / len(cuts)))
        gain = gain * jnp.repeat(draws, extent[axis_at] // parts).reshape([-1 if axis == axis_at else 1 for axis in range(len(extent))])
    return gain


def gaussian(rng, extent, width, most, pieces=(), held_as=jnp.bfloat16):
    factor_of = shard_levels(rng, extent, pieces, -0.22, 0.18) if pieces else 1.0
    array = jax.random.normal(rng, extent, jnp.float32) * width * factor_of
    return jnp.minimum(jnp.maximum(array, -most), most).astype(held_as)


def bell_draw_with(rng, extent, width, reach, cuts, heavy, kind=jnp.bfloat16):
    entries = width * jax.random.normal(rng, extent, jnp.float32)
    if cuts:
        entries = entries * shard_levels(rng, extent, cuts, -0.22, 0.18)
    return jnp.clip(spiked(entries, jax.random.fold_in(rng, 3), *heavy), -reach, reach).astype(kind)


def setup_inputs(seed: int = 0) -> dict:
    seeds = jax.random.split(jax.random.key(seed), 8)
    queries = draw_queries(jax.random.fold_in(seeds[7], 71), 0)
    keys = draw_keys(jax.random.fold_in(seeds[7], 71), 0)
    values = gaussian(seeds[2], (TOKENS, D), 1.0, 6.0, ((0, 16), (1, 16)))
    out_grad = bell_draw_with(seeds[3], (TOKENS, D), 1.0, 6.0, ((0, 16),), (0, 1, 16, 2.0))
    o_weight = gaussian(seeds[4], (D, D), D ** -0.5, 0.0625, ((0, 16), (1, 16)))
    exponents = with_ends(jax.random.randint(seeds[5], (D,), -2, 3), jax.random.fold_in(seeds[5], 1), -2, 2).astype(jnp.int32)
    valid_lengths = draw_valid_lengths(jax.random.fold_in(seeds[7], 71), 0)
    return dict(queries=queries, keys=keys, values=values, out_grad=out_grad, o_weight=o_weight, exponents=exponents, valid_lengths=valid_lengths)


def sylvester(count):
    labels = jnp.arange(count, dtype=jnp.int32)
    common = labels[:, None] & labels[None, :]
    parity = jnp.zeros((count, count), jnp.int32)
    for bit_number in range(count.bit_length() - 1):
        parity = parity ^ common >> bit_number & 1
    return (1 - 2 * parity).astype(jnp.float32)

def attention_probs(query_heads, key_heads, length):
    count = query_heads.shape[0]
    score_scale = 1.0 / math.sqrt(query_heads.shape[2])
    scores = jnp.einsum('thc,shc->hts', query_heads.astype(jnp.float32), key_heads.astype(jnp.float32)) * score_scale
    places = jnp.arange(count, dtype=jnp.int32)
    allowed = (places[None, :] <= places[:, None]) & (places[None, :] < length)
    scores = jnp.where(allowed[None, :, :], scores, -1e+30)
    top = lax.optimization_barrier(jnp.max(scores, axis=-1, keepdims=True))
    weights = jnp.exp(scores - top)
    return weights / lax.optimization_barrier(jnp.sum(weights, axis=-1, keepdims=True))

def rotate_all(blocks):
    table = sylvester(HEADS)
    mixed = jnp.einsum('gh,thc->tgc', table, blocks.astype(jnp.float32))
    return (mixed / math.sqrt(HEADS)).astype(jnp.bfloat16)

def reference(queries, keys, values, out_grad, o_weight, exponents, valid_lengths):
    query_blocks = queries.reshape(BLOCKS, TOK_DEV, HEADS, HEAD_DIM)
    key_blocks = keys.reshape(BLOCKS, TOK_DEV, HEADS, HEAD_DIM)
    value_blocks = values.reshape(BLOCKS, TOK_DEV, HEADS, HEAD_DIM)

    def forward(items):
        query_heads, key_heads, value_heads, length = items
        probs_low = attention_probs(query_heads, key_heads, length).astype(jnp.bfloat16)
        return jnp.einsum('hts,shc->thc', probs_low.astype(jnp.float32), value_heads.astype(jnp.float32)).astype(jnp.bfloat16)
    attended = lax.map(forward, (query_blocks, key_blocks, value_blocks, valid_lengths))
    rotated = rotate_all(attended.reshape(TOKENS, HEADS, HEAD_DIM)).reshape(TOKENS, D)
    channel_scale = jnp.exp2(exponents.astype(jnp.float32))
    projected = jnp.dot(out_grad, o_weight.T, preferred_element_type=jnp.float32)
    grad_rotated = (projected * channel_scale[None, :]).astype(jnp.bfloat16)
    grad_attended = rotate_all(grad_rotated.reshape(TOKENS, HEADS, HEAD_DIM))
    grad_blocks = grad_attended.reshape(BLOCKS, TOK_DEV, HEADS, HEAD_DIM)

    def backward(items):
        query_heads, key_heads, value_heads, length, grad_out = items
        probs = attention_probs(query_heads, key_heads, length)
        probs_low = probs.astype(jnp.bfloat16).astype(jnp.float32)
        grad_out_wide = grad_out.astype(jnp.float32)
        grad_value = jnp.einsum('hts,thc->shc', probs_low, grad_out_wide).astype(jnp.bfloat16)
        grad_probs = jnp.einsum('thc,shc->hts', grad_out_wide, value_heads.astype(jnp.float32))
        centre = lax.optimization_barrier(jnp.sum(probs * grad_probs, axis=-1, keepdims=True))
        grad_scores = (probs * (grad_probs - centre) / math.sqrt(HEAD_DIM)).astype(jnp.bfloat16).astype(jnp.float32)
        grad_query = jnp.einsum('hts,shc->thc', grad_scores, key_heads.astype(jnp.float32)).astype(jnp.bfloat16)
        grad_key = jnp.einsum('hts,thc->shc', grad_scores, query_heads.astype(jnp.float32)).astype(jnp.bfloat16)
        return (grad_query, grad_key, grad_value)
    grad_query, grad_key, grad_value = lax.map(backward, (query_blocks, key_blocks, value_blocks, valid_lengths, grad_blocks))

    def add_block(total, index):
        rows_rotated = lax.dynamic_slice_in_dim(rotated, (index * TOK_DEV).astype(jnp.int32), TOK_DEV, 0)
        rows_grad = lax.dynamic_slice_in_dim(out_grad, (index * TOK_DEV).astype(jnp.int32), TOK_DEV, 0)
        partial_value = jnp.dot(rows_rotated.T, rows_grad, preferred_element_type=jnp.float32)
        rounded = lax.optimization_barrier(partial_value.astype(jnp.bfloat16)).astype(jnp.float32)
        return (total + rounded, None)
    total, unused = lax.scan(add_block, jnp.zeros((D, D), jnp.float32), jnp.arange(BLOCKS, dtype=jnp.int32))
    grad_weight = total * channel_scale[:, None]
    return (grad_query.reshape(TOKENS, D), grad_key.reshape(TOKENS, D), grad_value.reshape(TOKENS, D), grad_weight)
```

```python
import functools
import math

import jax
import jax.numpy as jnp
from jax import lax
from jax.experimental import pallas as pl
from jax.experimental.pallas import tpu as pltpu
from jax.sharding import Mesh
from jax.sharding import PartitionSpec as P

HEADS = 64
HEAD_DIM = 128
DP = ("z", "xh")
TENSOR = ("y", "xl", "co")
BLK = 512
VMEM_LIMIT = 48 * 1024 * 1024


def params():
    return pltpu.CompilerParams(vmem_limit_bytes=VMEM_LIMIT)


def dot(a, b, ca, cb):
    return lax.dot_general(a, b, (((ca,), (cb,)), ((), ())), preferred_element_type=jnp.float32)


def fwd_kernel(len_ref, q_ref, k_ref, v_ref, att_ref, p_ref):
    scores = dot(q_ref[...], k_ref[...], 1, 1) * (1.0 / math.sqrt(HEAD_DIM))
    t = lax.broadcasted_iota(jnp.int32, scores.shape, 0)
    s = lax.broadcasted_iota(jnp.int32, scores.shape, 1)
    scores = jnp.where((s <= t) & (s < len_ref[0]), scores, -1e30)
    top = jnp.max(scores, axis=-1, keepdims=True)
    weights = jnp.exp(scores - top)
    probs = weights / jnp.sum(weights, axis=-1, keepdims=True)
    p_ref[0] = probs
    att_ref[...] = dot(probs.astype(jnp.bfloat16), v_ref[...], 1, 0).astype(jnp.bfloat16)


def attention_fwd(length, q, k, v):
    heads = q.shape[1] // HEAD_DIM
    head = pl.BlockSpec((BLK, HEAD_DIM), lambda h, *_: (0, h))
    return pl.pallas_call(
        fwd_kernel,
        grid_spec=pltpu.PrefetchScalarGridSpec(
            num_scalar_prefetch=1,
            grid=(heads,),
            in_specs=[head, head, head],
            out_specs=[head, pl.BlockSpec((1, BLK, BLK), lambda h, *_: (h, 0, 0))],
        ),
        out_shape=[
            jax.ShapeDtypeStruct(q.shape, jnp.bfloat16),
            jax.ShapeDtypeStruct((heads, BLK, BLK), jnp.float32),
        ],
        compiler_params=params(),
        cost_estimate=pl.CostEstimate(
            flops=heads * 4 * BLK * BLK * HEAD_DIM, bytes_accessed=8 << 20, transcendentals=heads * BLK * BLK
        ),
        name="attention_fwd",
    )(length, q, k, v)


def bwd_kernel(p_ref, q_ref, k_ref, v_ref, g_ref, dq_ref, dk_ref, dv_ref):
    probs = p_ref[0]
    grad = g_ref[...]
    dv_ref[...] = dot(probs.astype(jnp.bfloat16), grad, 0, 0).astype(jnp.bfloat16)
    grad_probs = dot(grad, v_ref[...], 1, 1)
    centre = jnp.sum(probs * grad_probs, axis=-1, keepdims=True)
    grad_scores = (probs * (grad_probs - centre) * (1.0 / math.sqrt(HEAD_DIM))).astype(jnp.bfloat16)
    dq_ref[...] = dot(grad_scores, k_ref[...], 1, 0).astype(jnp.bfloat16)
    dk_ref[...] = dot(grad_scores, q_ref[...], 0, 0).astype(jnp.bfloat16)


def attention_bwd(probs, q, k, v, grad):
    heads = q.shape[1] // HEAD_DIM
    head = pl.BlockSpec((BLK, HEAD_DIM), lambda h: (0, h))
    return pl.pallas_call(
        bwd_kernel,
        grid=(heads,),
        in_specs=[pl.BlockSpec((1, BLK, BLK), lambda h: (h, 0, 0)), head, head, head, head],
        out_specs=[head, head, head],
        out_shape=[jax.ShapeDtypeStruct(q.shape, jnp.bfloat16)] * 3,
        compiler_params=params(),
        cost_estimate=pl.CostEstimate(
            flops=heads * 8 * BLK * BLK * HEAD_DIM, bytes_accessed=8 << 20, transcendentals=0
        ),
        name="attention_bwd",
    )(probs, q, k, v, grad)


def pick_kernel(place_ref, o_ref, out_ref):
    out_ref[0] = o_ref[...]


def pick_blocks(place, out_grad):
    return pl.pallas_call(
        pick_kernel,
        grid_spec=pltpu.PrefetchScalarGridSpec(
            num_scalar_prefetch=1,
            grid=(4,),
            in_specs=[pl.BlockSpec((BLK, BLK), lambda i, p: (0, 2 * (4 * p[1] + i) + 1 - p[0]))],
            out_specs=pl.BlockSpec((1, BLK, BLK), lambda i, p: (i, 0, 0)),
        ),
        out_shape=jax.ShapeDtypeStruct((4, BLK, BLK), jnp.bfloat16),
        compiler_params=params(),
        name="pick_blocks",
    )(place, out_grad)


def near(i, p):
    return jnp.minimum(i, 3)


def far(i, p):
    return jnp.maximum(i - 4, 0)


def block_of(i, p):
    return lax.rem(4 * p[1] + i, 8)


def grad_kernel(place_ref, own_ref, near_ref, far_ref, w_ref, scale_ref, out_ref, acc_ref):
    i = pl.program_id(0)
    w = w_ref[...]

    @pl.when(i == 0)
    def _():
        acc_ref[...] = jnp.zeros_like(acc_ref)

    acc_ref[0] += dot(own_ref[...], w, 1, 1)

    @pl.when(i < 4)
    def _():
        acc_ref[1] += dot(near_ref[0], w, 1, 1)

    @pl.when(i >= 4)
    def _():
        acc_ref[1] += dot(far_ref[0], w, 1, 1)

    @pl.when(i == 7)
    def _():
        scale = scale_ref[...]
        x_hi = place_ref[0]
        out_ref[x_hi] = (acc_ref[0] * scale).astype(jnp.bfloat16)
        out_ref[1 - x_hi] = (acc_ref[1] * scale).astype(jnp.bfloat16)


def grad_dot(place, out_grad, near_blocks, far_blocks, weights, scale):
    return pl.pallas_call(
        grad_kernel,
        grid_spec=pltpu.PrefetchScalarGridSpec(
            num_scalar_prefetch=1,
            grid=(8,),
            in_specs=[
                pl.BlockSpec((BLK, BLK), lambda i, p: (0, 2 * block_of(i, p) + p[0])),
                pl.BlockSpec((1, BLK, BLK), lambda i, p: (near(i, p), 0, 0)),
                pl.BlockSpec((1, BLK, BLK), lambda i, p: (far(i, p), 0, 0)),
                pl.BlockSpec((BLK, BLK), lambda i, p: (block_of(i, p), 0)),
                pl.BlockSpec((1, BLK), lambda i, p: (0, 0)),
            ],
            out_specs=pl.BlockSpec((2, BLK, BLK), lambda i, p: (0, 0, 0)),
            scratch_shapes=[pltpu.VMEM((2, BLK, BLK), jnp.float32)],
        ),
        out_shape=jax.ShapeDtypeStruct((2, BLK, BLK), jnp.bfloat16),
        compiler_params=params(),
        cost_estimate=pl.CostEstimate(
            flops=4 * BLK * BLK * BLK * 8, bytes_accessed=13 << 20, transcendentals=0
        ),
        name="grad_dot",
    )(place, out_grad, near_blocks, far_blocks, weights, scale)


def weight_kernel(place_ref, a_ref, b_ref, own_ref, near_ref, far_ref, out_ref, at_ref, bt_ref):
    i = pl.program_id(0)

    @pl.when(i == 0)
    def _():
        at_ref[...] = a_ref[...].T
        bt_ref[...] = b_ref[...].T

    mine = dot(at_ref[...], own_ref[...], 1, 0)

    @pl.when(i < 4)
    def _():
        out_ref[...] = (mine + dot(bt_ref[...], near_ref[0], 1, 0)).astype(jnp.bfloat16)

    @pl.when(i >= 4)
    def _():
        out_ref[...] = (mine + dot(bt_ref[...], far_ref[0], 1, 0)).astype(jnp.bfloat16)


def weight_dot(place, rotated, rotated_other, out_grad, near_blocks, far_blocks):
    whole = pl.BlockSpec((BLK, BLK), lambda i, p: (0, 0))
    return pl.pallas_call(
        weight_kernel,
        grid_spec=pltpu.PrefetchScalarGridSpec(
            num_scalar_prefetch=1,
            grid=(8,),
            in_specs=[
                whole,
                whole,
                pl.BlockSpec((BLK, BLK), lambda i, p: (0, 2 * block_of(i, p) + p[0])),
                pl.BlockSpec((1, BLK, BLK), lambda i, p: (near(i, p), 0, 0)),
                pl.BlockSpec((1, BLK, BLK), lambda i, p: (far(i, p), 0, 0)),
            ],
            out_specs=pl.BlockSpec((BLK, BLK), lambda i, p: (block_of(i, p), 0)),
            scratch_shapes=[pltpu.VMEM((BLK, BLK), jnp.bfloat16)] * 2,
        ),
        out_shape=jax.ShapeDtypeStruct((8 * BLK, BLK), jnp.bfloat16),
        compiler_params=params(),
        cost_estimate=pl.CostEstimate(
            flops=4 * BLK * BLK * BLK * 8, bytes_accessed=13 << 20, transcendentals=0
        ),
        name="weight_dot",
    )(place, rotated, rotated_other, out_grad, near_blocks, far_blocks)


def mix_kernel(parts, x_ref, out_ref):
    x = x_ref[...].astype(jnp.float32)
    rows = x.shape[0] // parts
    total = x[:rows]
    for part in range(1, parts):
        total = total + x[part * rows : (part + 1) * rows]
    tokens = rows // 16
    blocks = [
        [total[s * tokens : (s + 1) * tokens, c * HEAD_DIM : (c + 1) * HEAD_DIM] for c in range(4)]
        for s in range(16)
    ]
    flat = [blocks[s][c] for s in range(16) for c in range(4)]
    step = 1
    while step < 64:
        flat = [
            flat[i] + flat[i + step] if not i & step else flat[i - step] - flat[i]
            for i in range(64)
        ]
        step *= 2
    for s in range(16):
        for c in range(4):
            out_ref[s * tokens : (s + 1) * tokens, c * HEAD_DIM : (c + 1) * HEAD_DIM] = (
                flat[s * 4 + c] * (1.0 / math.sqrt(HEADS))
            ).astype(jnp.bfloat16)


def mix(x, parts):
    return pl.pallas_call(
        functools.partial(mix_kernel, parts),
        out_shape=jax.ShapeDtypeStruct((x.shape[0] // parts, x.shape[1]), jnp.bfloat16),
        compiler_params=params(),
        name="mix",
    )(x)


def body(queries, keys, values, out_grad, o_weight, exponents, valid_lengths):
    x_hi, core = lax.axis_index("xh"), lax.axis_index("co")
    place = jnp.stack([x_hi, core]).astype(jnp.int32)
    scale = jnp.exp2(exponents.astype(jnp.float32))

    weights = lax.all_gather(o_weight, "z", axis=0, tiled=True)
    across = [((h * 2 + l), (1 - h) * 2 + 1 - l) for h in range(2) for l in range(2)]
    near_blocks = lax.ppermute(pick_blocks(place, out_grad), ("xh", "xl"), across)
    far_blocks = lax.ppermute(near_blocks, "co", [(0, 1), (1, 0)])

    attended, probs = attention_fwd(valid_lengths, queries, keys, values)
    turned = lax.all_to_all(attended, TENSOR, 0, 0, tiled=True)
    rotated = lax.all_to_all(mix(turned, 1), TENSOR, 0, 0, tiled=True)
    rotated_other = lax.ppermute(rotated, "xh", [(0, 1), (1, 0)])
    partial = weight_dot(place, rotated, rotated_other, out_grad, near_blocks, far_blocks)
    summed = lax.psum_scatter(partial, "z", scatter_dimension=0, tiled=True)

    grad_rotated = grad_dot(place, out_grad, near_blocks, far_blocks, weights, scale[None, :])
    turned = lax.all_to_all(grad_rotated.reshape(2 * BLK, BLK), ("xh",) + TENSOR, 0, 0, tiled=True)
    grad_attended = lax.all_to_all(mix(turned, 2), TENSOR, 0, 0, tiled=True)
    grad_query, grad_key, grad_value = attention_bwd(probs, queries, keys, values, grad_attended)

    grad_weight = summed.astype(jnp.float32) * scale[:, None]
    return grad_query, grad_key, grad_value, grad_weight


def solution(mesh):
    fine = Mesh(mesh.devices.reshape(8, 2, 4, 2, 2), DP + TENSOR)
    return jax.shard_map(
        body,
        mesh=fine,
        in_specs=(
            P(DP, TENSOR),
            P(DP, TENSOR),
            P(DP, TENSOR),
            P(DP, None),
            P(TENSOR, DP),
            P(TENSOR),
            P(DP),
        ),
        out_specs=(P(DP, TENSOR), P(DP, TENSOR), P(DP, TENSOR), P(TENSOR, DP)),
        check_vma=False,
    )
```

```python
import functools
import math

import jax
import jax.numpy as jnp
from jax import lax
from jax.experimental import pallas as pl
from jax.experimental.pallas import tpu as pltpu
from jax.sharding import Mesh
from jax.sharding import PartitionSpec as P

HEADS = 64
HEAD_DIM = 128
DP = ("z", "xh")
TENSOR = ("y", "xl", "co")
BLK = 512


def params(mib=60):
    return pltpu.CompilerParams(vmem_limit_bytes=mib * 1024 * 1024)


def dot(a, b, ca, cb):
    return lax.dot_general(a, b, (((ca,), (cb,)), ((), ())), preferred_element_type=jnp.float32)


def fwd_kernel(len_ref, q_ref, k_ref, v_ref, att_ref, p_ref):
    scores = dot(q_ref[...], k_ref[...], 1, 1) * (1.0 / math.sqrt(HEAD_DIM))
    t = lax.broadcasted_iota(jnp.int32, scores.shape, 0)
    s = lax.broadcasted_iota(jnp.int32, scores.shape, 1)
    scores = jnp.where((s <= t) & (s < len_ref[0]), scores, -1e30)
    top = jnp.max(scores, axis=-1, keepdims=True)
    weights = jnp.exp(scores - top)
    probs = weights / jnp.sum(weights, axis=-1, keepdims=True)
    p_ref[0] = probs
    att_ref[...] = dot(probs.astype(jnp.bfloat16), v_ref[...], 1, 0).astype(jnp.bfloat16)


def attention_fwd(length, q, k, v):
    heads = q.shape[1] // HEAD_DIM
    head = pl.BlockSpec((BLK, HEAD_DIM), lambda h, *_: (0, h))
    return pl.pallas_call(
        fwd_kernel,
        grid_spec=pltpu.PrefetchScalarGridSpec(
            num_scalar_prefetch=1,
            grid=(heads,),
            in_specs=[head, head, head],
            out_specs=[head, pl.BlockSpec((1, BLK, BLK), lambda h, *_: (h, 0, 0))],
        ),
        out_shape=[
            jax.ShapeDtypeStruct(q.shape, jnp.bfloat16),
            jax.ShapeDtypeStruct((heads, BLK, BLK), jnp.float32),
        ],
        compiler_params=params(),
        cost_estimate=pl.CostEstimate(
            flops=heads * 4 * BLK * BLK * HEAD_DIM, bytes_accessed=8 << 20, transcendentals=heads * BLK * BLK
        ),
        name="attention_fwd",
    )(length, q, k, v)


def bwd_kernel(p_ref, q_ref, k_ref, v_ref, g_ref, dq_ref, dk_ref, dv_ref):
    probs = p_ref[0]
    grad = g_ref[...]
    dv_ref[...] = dot(probs.astype(jnp.bfloat16), grad, 0, 0).astype(jnp.bfloat16)
    grad_probs = dot(grad, v_ref[...], 1, 1)
    centre = jnp.sum(probs * grad_probs, axis=-1, keepdims=True)
    grad_scores = (probs * (grad_probs - centre) * (1.0 / math.sqrt(HEAD_DIM))).astype(jnp.bfloat16)
    dq_ref[...] = dot(grad_scores, k_ref[...], 1, 0).astype(jnp.bfloat16)
    dk_ref[...] = dot(grad_scores, q_ref[...], 0, 0).astype(jnp.bfloat16)


def attention_bwd(probs, q, k, v, grad):
    heads = q.shape[1] // HEAD_DIM
    head = pl.BlockSpec((BLK, HEAD_DIM), lambda h: (0, h))
    return pl.pallas_call(
        bwd_kernel,
        grid=(heads,),
        in_specs=[pl.BlockSpec((1, BLK, BLK), lambda h: (h, 0, 0)), head, head, head, head],
        out_specs=[head, head, head],
        out_shape=[jax.ShapeDtypeStruct(q.shape, jnp.bfloat16)] * 3,
        compiler_params=params(),
        cost_estimate=pl.CostEstimate(
            flops=heads * 8 * BLK * BLK * HEAD_DIM, bytes_accessed=8 << 20, transcendentals=0
        ),
        name="attention_bwd",
    )(probs, q, k, v, grad)


PIECES = ((0, 3), (3, 3), (6, 1), (7, 1))


def block_of(i, p):
    core = jnp.where((i < 3) | (i == 6), p[1], 1 - p[1])
    return 4 * core + jnp.where(i < 6, p[2] + lax.rem(i, 3), 3 * (1 - p[2]))


ANY = pl.BlockSpec(memory_space=pl.ANY)
SMEM = pl.BlockSpec(memory_space=pltpu.SMEM)
VMEM = pl.BlockSpec(memory_space=pltpu.VMEM)


def place_of(place_ref):
    return place_ref[0], place_ref[1], place_ref[2]


def own_copy(grad_ref, place, buf, sems):
    def copy(i):
        column = pl.multiple_of((2 * block_of(i, place) + place[0]) * BLK, BLK)
        return pltpu.make_async_copy(grad_ref.at[:, pl.ds(column, BLK)], buf.at[i], sems.at[i])

    return copy


def row_copy(ref, buf, sems, index=lambda i: i, out=False):
    def copy(i):
        rows = ref.at[pl.ds(pl.multiple_of(index(i) * BLK, BLK), BLK)]
        if out:
            return pltpu.make_async_copy(buf.at[i], rows, sems.at[i])
        return pltpu.make_async_copy(rows, buf.at[i], sems.at[i])

    return copy


def piece_copies(refs, buf, sems):
    return [
        pltpu.make_async_copy(ref, buf.at[pl.ds(first, count)], sems.at[at])
        for at, (ref, (first, count)) in enumerate(zip(refs, PIECES))
    ]


def each(first, count, step):
    def body(i, carry):
        step(i)
        return carry

    lax.fori_loop(first, first + count, body, 0)


def grad_kernel(place_ref, grad_ref, near, far, last, far_last, w_ref, scale_ref, out_ref, *scratch):
    own_buf, w_buf, piece_buf, acc_ref, own_sems, w_sems, piece_sems = scratch
    place = place_of(place_ref)
    own = own_copy(grad_ref, place, own_buf, own_sems)
    weight = row_copy(w_ref, w_buf, w_sems, lambda i: block_of(i, place))
    pieces = piece_copies((near, far, last, far_last), piece_buf, piece_sems)
    own(0).start()
    weight(0).start()
    pieces[0].start()

    def begin(i):
        own(i).start()
        weight(i).start()

    each(1, 7, begin)
    for piece in pieces[1:]:
        piece.start()
    acc_ref[...] = jnp.zeros_like(acc_ref)

    def step(i):
        own(i).wait()
        weight(i).wait()
        w = w_buf[i]
        acc_ref[0] += dot(own_buf[i], w, 1, 1)
        acc_ref[1] += dot(piece_buf[i], w, 1, 1)

    for piece, (first, count) in zip(pieces, PIECES):
        piece.wait()
        each(first, count, step)
    scale = scale_ref[...]
    x_hi = place[0]
    out_ref[x_hi] = (acc_ref[0] * scale).astype(jnp.bfloat16)
    out_ref[1 - x_hi] = (acc_ref[1] * scale).astype(jnp.bfloat16)


def grad_dot(place, out_grad, pieces, weights, scale):
    blocks = pltpu.VMEM((8, BLK, BLK), jnp.bfloat16)
    return pl.pallas_call(
        grad_kernel,
        in_specs=[SMEM, ANY, *[ANY] * 4, ANY, VMEM],
        out_specs=VMEM,
        scratch_shapes=[
            blocks,
            blocks,
            blocks,
            pltpu.VMEM((2, BLK, BLK), jnp.float32),
            pltpu.SemaphoreType.DMA((8,)),
            pltpu.SemaphoreType.DMA((8,)),
            pltpu.SemaphoreType.DMA((4,)),
        ],
        out_shape=jax.ShapeDtypeStruct((2, BLK, BLK), jnp.bfloat16),
        compiler_params=params(60),
        cost_estimate=pl.CostEstimate(
            flops=4 * BLK * BLK * BLK * 8, bytes_accessed=13 << 20, transcendentals=0
        ),
        name="grad_dot",
    )(place, out_grad, *pieces, weights, scale)


def own_kernel(place_ref, a_ref, grad_ref, out_ref, at_ref, in_buf, out_buf, in_sems, out_sems):
    place = place_of(place_ref)
    own = own_copy(grad_ref, place, in_buf, in_sems)
    out = row_copy(out_ref, out_buf, out_sems, out=True)
    each(0, 8, lambda i: own(i).start())
    at_ref[...] = a_ref[...].T

    def step(i):
        own(i).wait()
        out_buf[i] = dot(at_ref[...], in_buf[i], 1, 0).astype(jnp.bfloat16)
        out(i).start()

    each(0, 8, step)
    each(0, 8, lambda i: out(i).wait())


def own_dot(place, rotated, out_grad):
    blocks = pltpu.VMEM((8, BLK, BLK), jnp.bfloat16)
    return pl.pallas_call(
        own_kernel,
        in_specs=[SMEM, VMEM, ANY],
        out_specs=ANY,
        scratch_shapes=[
            pltpu.VMEM((BLK, BLK), jnp.bfloat16),
            blocks,
            blocks,
            pltpu.SemaphoreType.DMA((8,)),
            pltpu.SemaphoreType.DMA((8,)),
        ],
        out_shape=jax.ShapeDtypeStruct((8 * BLK, BLK), jnp.bfloat16),
        compiler_params=params(60),
        cost_estimate=pl.CostEstimate(
            flops=2 * BLK * BLK * BLK * 8, bytes_accessed=9 << 20, transcendentals=0
        ),
        name="own_dot",
    )(place, rotated, out_grad)


def other_kernel(place_ref, a_ref, own_ref, near, far, last, far_last, out_ref, *scratch):
    at_ref, own_buf, piece_buf, out_buf, own_sems, piece_sems, out_sems = scratch
    place = place_of(place_ref)
    own = row_copy(own_ref, own_buf, own_sems)
    pieces = piece_copies((near, far, last, far_last), piece_buf, piece_sems)
    out = row_copy(out_ref, out_buf, out_sems, lambda i: block_of(i, place), out=True)
    pieces[0].start()
    each(0, 8, lambda i: own(i).start())
    for piece in pieces[1:]:
        piece.start()
    at_ref[...] = a_ref[...].T

    def step(i):
        own(i).wait()
        total = own_buf[i].astype(jnp.float32) + dot(at_ref[...], piece_buf[i], 1, 0)
        out_buf[i] = total.astype(jnp.bfloat16)
        out(i).start()

    for piece, (first, count) in zip(pieces, PIECES):
        piece.wait()
        each(first, count, step)
    each(0, 8, lambda i: out(i).wait())


def other_dot(place, rotated, own, pieces):
    blocks = pltpu.VMEM((8, BLK, BLK), jnp.bfloat16)
    return pl.pallas_call(
        other_kernel,
        in_specs=[SMEM, VMEM, ANY, *[ANY] * 4],
        out_specs=ANY,
        scratch_shapes=[
            pltpu.VMEM((BLK, BLK), jnp.bfloat16),
            blocks,
            blocks,
            blocks,
            pltpu.SemaphoreType.DMA((8,)),
            pltpu.SemaphoreType.DMA((4,)),
            pltpu.SemaphoreType.DMA((8,)),
        ],
        out_shape=jax.ShapeDtypeStruct((8 * BLK, BLK), jnp.bfloat16),
        compiler_params=params(60),
        cost_estimate=pl.CostEstimate(
            flops=2 * BLK * BLK * BLK * 8, bytes_accessed=13 << 20, transcendentals=0
        ),
        name="other_dot",
    )(place, rotated, own, *pieces)


def mix_kernel(parts, copies, x_ref, out_ref):
    x = x_ref[...].astype(jnp.float32)
    rows = x.shape[0] // parts
    total = x[:rows]
    for part in range(1, parts):
        total = total + x[part * rows : (part + 1) * rows]
    tokens = rows // 16
    blocks = [
        [total[s * tokens : (s + 1) * tokens, c * HEAD_DIM : (c + 1) * HEAD_DIM] for c in range(4)]
        for s in range(16)
    ]
    flat = [blocks[s][c] for s in range(16) for c in range(4)]
    step = 1
    while step < 64:
        flat = [
            flat[i] + flat[i + step] if not i & step else flat[i - step] - flat[i]
            for i in range(64)
        ]
        step *= 2
    for s in range(16):
        for c in range(4):
            mixed = (flat[s * 4 + c] * (1.0 / math.sqrt(HEADS))).astype(jnp.bfloat16)
            for copy in range(copies):
                first = copy * rows + s * tokens
                out_ref[first : first + tokens, c * HEAD_DIM : (c + 1) * HEAD_DIM] = mixed


def mix(x, parts, copies):
    return pl.pallas_call(
        functools.partial(mix_kernel, parts, copies),
        out_shape=jax.ShapeDtypeStruct((x.shape[0] // parts * copies, x.shape[1]), jnp.bfloat16),
        compiler_params=params(16),
        name="mix",
    )(x)


def body(queries, keys, values, out_grad, o_weight, exponents, valid_lengths):
    x_hi, core, y = (lax.axis_index(name) for name in ("xh", "co", "y"))
    y_bit = lax.rem(y, 2)
    place = jnp.stack([x_hi, core, y_bit]).astype(jnp.int32)
    scale = jnp.exp2(exponents.astype(jnp.float32))

    weights = lax.all_gather(o_weight, "z", axis=0, tiled=True)

    across = [(h * 2 + l, (1 - h) * 2 + 1 - l) for h in range(2) for l in range(2)]
    swap, pairs = [(0, 1), (1, 0)], [(0, 1), (1, 0), (2, 3), (3, 2)]
    picked = jnp.stack(
        [
            lax.dynamic_slice(out_grad, (0, (2 * (4 * core + y_bit + i) + 1 - x_hi) * BLK), (BLK, BLK))
            for i in range(3)
        ]
    )
    near = lax.ppermute(picked, ("xh", "xl"), across)

    queries, _ = lax.optimization_barrier((queries, picked))
    attended, probs = attention_fwd(valid_lengths, queries, keys, values)
    turned = lax.all_to_all(attended, TENSOR, 0, 0, tiled=True)
    rotated = lax.all_to_all(mix(turned, 1, 1), TENSOR, 0, 0, tiled=True)
    rotated_other = lax.ppermute(rotated, "xh", swap)
    near, rotated = lax.optimization_barrier((near, rotated))
    last = lax.ppermute(lax.dynamic_slice(near, (2 * y_bit, 0, 0), (1, BLK, BLK)), "y", pairs)
    far = lax.ppermute(near, "co", swap)
    own = own_dot(place, rotated, out_grad)
    last, own = lax.optimization_barrier((last, own))
    far_last = lax.ppermute(last, "co", swap)
    pieces = [near, far, last, far_last]
    partial = other_dot(place, rotated_other, own, pieces)
    summed = lax.psum_scatter(partial, "z", scatter_dimension=0, tiled=True)

    grad_rotated = grad_dot(place, out_grad, pieces, weights, scale[None, :])
    turned = lax.all_to_all(grad_rotated.reshape(2 * BLK, BLK), ("xh",) + TENSOR, 0, 0, tiled=True)
    grad_attended = lax.all_to_all(mix(turned, 2, 1), TENSOR, 0, 0, tiled=True)
    grad_query, grad_key, grad_value = attention_bwd(probs, queries, keys, values, grad_attended)

    grad_weight = summed.astype(jnp.float32) * scale[:, None]
    return grad_query, grad_key, grad_value, grad_weight


def solution(mesh):
    fine = Mesh(mesh.devices.reshape(8, 2, 4, 2, 2), DP + TENSOR)
    return jax.shard_map(
        body,
        mesh=fine,
        in_specs=(
            P(DP, TENSOR),
            P(DP, TENSOR),
            P(DP, TENSOR),
            P(DP, None),
            P(TENSOR, DP),
            P(TENSOR),
            P(DP),
        ),
        out_specs=(P(DP, TENSOR), P(DP, TENSOR), P(DP, TENSOR), P(TENSOR, DP)),
        check_vma=False,
    )
```

```python
import functools
import math

import jax
import jax.numpy as jnp
from jax import lax
from jax.experimental import pallas as pl
from jax.experimental.pallas import tpu as pltpu
from jax.sharding import Mesh
from jax.sharding import PartitionSpec as P

HEADS = 64
HEAD_DIM = 128
DP = ("z", "xh")
TENSOR = ("y", "xl", "co")
BLK = 512


ANY = pl.BlockSpec(memory_space=pl.ANY)
HBM = pl.BlockSpec(memory_space=pltpu.HBM)
SMEM = pl.BlockSpec(memory_space=pltpu.SMEM)
VMEM = pl.BlockSpec(memory_space=pltpu.VMEM)
FWD, BWD = 24, 24
OVER_X = 6
OVER_Y = 8 - OVER_X


def params(mib=60):
    return pltpu.CompilerParams(vmem_limit_bytes=mib * 1024 * 1024)


def dot(a, b, ca, cb):
    return lax.dot_general(a, b, (((ca,), (cb,)), ((), ())), preferred_element_type=jnp.float32)


HALF = BLK // 2


def fwd_kernel(len_ref, q_ref, k_ref, v_ref, att_ref, p_ref):
    for head in range(p_ref.shape[0]):
        cols = slice(head * HEAD_DIM, (head + 1) * HEAD_DIM)
        for first, keys in ((0, HALF), (HALF, BLK)):
            rows = slice(first, first + HALF)
            scores = dot(q_ref[rows, cols], k_ref[:keys, cols], 1, 1) * (1.0 / math.sqrt(HEAD_DIM))
            t = first + lax.broadcasted_iota(jnp.int32, scores.shape, 0)
            s = lax.broadcasted_iota(jnp.int32, scores.shape, 1)
            scores = jnp.where(s < jnp.minimum(t + 1, len_ref[0]), scores, -1e30)
            top = jnp.max(scores, axis=-1, keepdims=True)
            weights = jnp.exp(scores - top)
            probs = (weights * (1.0 / jnp.sum(weights, axis=-1, keepdims=True))).astype(jnp.bfloat16)
            p_ref[head, rows, :keys] = probs
            att_ref[rows, cols] = dot(probs, v_ref[:keys, cols], 1, 0).astype(jnp.bfloat16)


def attention_fwd(length, q, k, v):
    heads = q.shape[1] // HEAD_DIM
    return pl.pallas_call(
        fwd_kernel,
        in_specs=[SMEM, VMEM, VMEM, VMEM],
        out_specs=[VMEM, VMEM],
        out_shape=[
            jax.ShapeDtypeStruct(q.shape, jnp.bfloat16),
            jax.ShapeDtypeStruct((heads, BLK, BLK), jnp.bfloat16),
        ],
        compiler_params=params(FWD),
        cost_estimate=pl.CostEstimate(
            flops=heads * 4 * BLK * BLK * HEAD_DIM, bytes_accessed=6 << 20, transcendentals=heads * BLK * BLK
        ),
        name="attention_fwd",
    )(length, q, k, v)


def bwd_kernel(p_ref, q_ref, k_ref, v_ref, g_ref, dq_ref, dk_ref, dv_ref):
    for head in range(p_ref.shape[0]):
        cols = slice(head * HEAD_DIM, (head + 1) * HEAD_DIM)
        grad_keys, grad_values = [], []
        for first, keys in ((0, HALF), (HALF, BLK)):
            rows = slice(first, first + HALF)
            probs, grad = p_ref[head, rows, :keys], g_ref[rows, cols]
            grad_values.append(dot(probs, grad, 0, 0))
            grad_probs = dot(grad, v_ref[:keys, cols], 1, 1)
            wide = probs.astype(jnp.float32)
            centre = jnp.sum(wide * grad_probs, axis=-1, keepdims=True)
            grad_scores = (wide * (grad_probs - centre) * (1.0 / math.sqrt(HEAD_DIM))).astype(jnp.bfloat16)
            dq_ref[rows, cols] = dot(grad_scores, k_ref[:keys, cols], 1, 0).astype(jnp.bfloat16)
            grad_keys.append(dot(grad_scores, q_ref[rows, cols], 0, 0))
        for ref, (early, late) in ((dk_ref, grad_keys), (dv_ref, grad_values)):
            ref[:HALF, cols] = (early + late[:HALF]).astype(jnp.bfloat16)
            ref[HALF:, cols] = late[HALF:].astype(jnp.bfloat16)


def attention_bwd(probs, q, k, v, grad):
    heads = q.shape[1] // HEAD_DIM
    return pl.pallas_call(
        bwd_kernel,
        in_specs=[VMEM] * 5,
        out_specs=[VMEM] * 3,
        out_shape=[jax.ShapeDtypeStruct(q.shape, jnp.bfloat16)] * 3,
        compiler_params=params(BWD),
        cost_estimate=pl.CostEstimate(
            flops=heads * 8 * BLK * BLK * HEAD_DIM, bytes_accessed=6 << 20, transcendentals=0
        ),
        name="attention_bwd",
    )(probs, q, k, v, grad)


def unit_of(v, y_bit):
    return jnp.where(y_bit == 0, v, 7 - v)


def block_of(i, p):
    return 4 * jnp.where(i < 4, p[1], 1 - p[1]) + lax.rem(i, 4)


def place_here():
    return lax.axis_index("xh"), lax.axis_index("co"), lax.rem(lax.axis_index("y"), 2)


def own_copy(grad_ref, place, buf, sems):
    def copy(i):
        column = pl.multiple_of((2 * block_of(i, place) + place[0]) * BLK, BLK)
        return pltpu.make_async_copy(grad_ref.at[:, pl.ds(column, BLK)], buf.at[i], sems.at[i])

    return copy


def row_copy(ref, buf, sems, index=lambda i: i, out=False):
    def copy(i):
        rows = ref.at[pl.ds(pl.multiple_of(index(i) * BLK, BLK), BLK)]
        if out:
            return pltpu.make_async_copy(buf.at[i], rows, sems.at[i])
        return pltpu.make_async_copy(rows, buf.at[i], sems.at[i])

    return copy


def piece_copies(refs, buf, sems, place):
    def target(group, v):
        unit = unit_of(v, place[2])
        rows = pl.ds(pl.multiple_of(lax.rem(unit, 2) * HALF, HALF), HALF)
        return buf.at[4 * group + unit // 2, rows]

    def start(group):
        over_x, over_y = refs[2 * group], refs[2 * group + 1]

        def begin(v):
            pltpu.make_async_copy(over_x.at[v], target(group, v), sems.at[8 * group + v]).start()

        each(0, OVER_X, begin)
        for w in range(OVER_Y):
            pltpu.make_async_copy(over_y.at[w], target(group, 7 - w), sems.at[8 * group + 7 - w]).start()

    def wait(i):
        group = i // 4
        for half in range(2):
            v = unit_of(2 * lax.rem(i, 4) + half, place[2])
            there = target(group, v)
            pltpu.make_async_copy(there, there, sems.at[8 * group + v]).wait()

    return start, wait, target


def each(first, count, step):
    def body(i, carry):
        step(i)
        return carry

    lax.fori_loop(first, first + count, body, 0)


def pick_kernel(grad_ref, out_ref, sems):
    x_hi, core, y_bit = place_here()

    def copy(v):
        unit = unit_of(v, y_bit)
        rows = pl.ds(pl.multiple_of(lax.rem(unit, 2) * HALF, HALF), HALF)
        column = pl.multiple_of((2 * (4 * core + unit // 2) + 1 - x_hi) * BLK, BLK)
        return pltpu.make_async_copy(grad_ref.at[rows, pl.ds(column, BLK)], out_ref.at[v], sems.at[v])

    each(0, OVER_X, lambda v: copy(v).start())
    each(0, OVER_X, lambda v: copy(v).wait())


def pick_units(out_grad):
    return pl.pallas_call(
        pick_kernel,
        in_specs=[HBM],
        out_specs=VMEM,
        scratch_shapes=[pltpu.SemaphoreType.DMA((OVER_X,))],
        out_shape=jax.ShapeDtypeStruct((OVER_X, HALF, BLK), jnp.bfloat16),
        compiler_params=params(60),
        name="pick_units",
    )(out_grad)


def grad_kernel(grad_ref, near, far, last_ref, w_ref, scale_ref, out_ref, *scratch):
    own_buf, w_buf, piece_buf, acc_ref, own_sems, w_sems, piece_sems = scratch
    place = place_here()
    own = own_copy(grad_ref, place, own_buf, own_sems)
    weight = row_copy(w_ref, w_buf, w_sems, lambda i: block_of(i, place))
    last = [last_ref.at[pl.ds(group * OVER_Y, OVER_Y)] for group in range(2)]
    start, wait, _ = piece_copies((near, last[0], far, last[1]), piece_buf, piece_sems, place)
    own(0).start()
    weight(0).start()
    start(0)

    def begin(i):
        own(i).start()
        weight(i).start()

    each(1, 7, begin)
    start(1)
    acc_ref[...] = jnp.zeros_like(acc_ref)

    def step(i):
        own(i).wait()
        weight(i).wait()
        wait(i)
        w = w_buf[i]
        acc_ref[0] += dot(own_buf[i], w, 1, 1)
        acc_ref[1] += dot(piece_buf[i], w, 1, 1)

    each(0, 8, step)
    scale = scale_ref[...]
    x_hi = place[0]
    out_ref[x_hi] = (acc_ref[0] * scale).astype(jnp.bfloat16)
    out_ref[1 - x_hi] = (acc_ref[1] * scale).astype(jnp.bfloat16)


def grad_dot(out_grad, near, far, last, weights, scale):
    blocks = pltpu.VMEM((8, BLK, BLK), jnp.bfloat16)
    return pl.pallas_call(
        grad_kernel,
        in_specs=[HBM, ANY, ANY, ANY, HBM, VMEM],
        out_specs=VMEM,
        scratch_shapes=[
            blocks,
            blocks,
            blocks,
            pltpu.VMEM((2, BLK, BLK), jnp.float32),
            pltpu.SemaphoreType.DMA((8,)),
            pltpu.SemaphoreType.DMA((8,)),
            pltpu.SemaphoreType.DMA((16,)),
        ],
        out_shape=jax.ShapeDtypeStruct((2, BLK, BLK), jnp.bfloat16),
        compiler_params=params(54),
        cost_estimate=pl.CostEstimate(
            flops=4 * BLK * BLK * BLK * 8, bytes_accessed=13 << 20, transcendentals=0
        ),
        name="grad_dot",
    )(out_grad, near, far, last, weights, scale)


def own_kernel(a_ref, grad_ref, out_ref, at_ref, in_buf, out_buf, in_sems, out_sems):
    place = place_here()
    own = own_copy(grad_ref, place, in_buf, in_sems)
    out = row_copy(out_ref, out_buf, out_sems, out=True)
    each(0, 8, lambda i: own(i).start())
    at_ref[...] = a_ref[...].T

    def step(i):
        own(i).wait()
        out_buf[i] = dot(at_ref[...], in_buf[i], 1, 0).astype(jnp.bfloat16)
        out(i).start()

    each(0, 8, step)
    each(0, 8, lambda i: out(i).wait())


def own_dot(rotated, out_grad):
    blocks = pltpu.VMEM((8, BLK, BLK), jnp.bfloat16)
    return pl.pallas_call(
        own_kernel,
        in_specs=[VMEM, HBM],
        out_specs=ANY,
        scratch_shapes=[
            pltpu.VMEM((BLK, BLK), jnp.bfloat16),
            blocks,
            blocks,
            pltpu.SemaphoreType.DMA((8,)),
            pltpu.SemaphoreType.DMA((8,)),
        ],
        out_shape=jax.ShapeDtypeStruct((8 * BLK, BLK), jnp.bfloat16),
        compiler_params=params(24),
        cost_estimate=pl.CostEstimate(
            flops=2 * BLK * BLK * BLK * 8, bytes_accessed=9 << 20, transcendentals=0
        ),
        name="own_dot",
    )(rotated, out_grad)


def other_kernel(a_ref, own_ref, near, last, far, far_last, out_ref, keep_ref, *scratch):
    at_ref, own_buf, piece_buf, out_buf, own_sems, piece_sems, out_sems, a_sem, keep_sems = scratch
    place = place_here()
    load = pltpu.make_async_copy(a_ref, at_ref, a_sem)
    load.start()
    own = row_copy(own_ref, own_buf, own_sems)
    start, wait, target = piece_copies((near, last, far, far_last), piece_buf, piece_sems, place)
    out = row_copy(out_ref, out_buf, out_sems, lambda i: block_of(i, place), out=True)
    start(0)
    each(0, 8, lambda i: own(i).start())
    start(1)
    load.wait()
    at_ref[...] = at_ref[...].T

    def step(i):
        own(i).wait()
        wait(i)
        total = own_buf[i].astype(jnp.float32) + dot(at_ref[...], piece_buf[i], 1, 0)
        out_buf[i] = total.astype(jnp.bfloat16)
        out(i).start()

    keeps = []
    for group in range(2):
        each(4 * group, 4, step)
        for w in range(OVER_Y):
            at = group * OVER_Y + w
            keeps.append(pltpu.make_async_copy(target(group, 7 - w), keep_ref.at[at], keep_sems.at[at]))
            keeps[-1].start()
    each(0, 8, lambda i: out(i).wait())
    for keep in keeps:
        keep.wait()


def other_dot(rotated, own, near, last, far, far_last):
    blocks = pltpu.VMEM((8, BLK, BLK), jnp.bfloat16)
    return pl.pallas_call(
        other_kernel,
        in_specs=[ANY, ANY, *[ANY] * 4],
        out_specs=[HBM, HBM],
        scratch_shapes=[
            pltpu.VMEM((BLK, BLK), jnp.bfloat16),
            blocks,
            blocks,
            blocks,
            pltpu.SemaphoreType.DMA((8,)),
            pltpu.SemaphoreType.DMA((16,)),
            pltpu.SemaphoreType.DMA((8,)),
            pltpu.SemaphoreType.DMA,
            pltpu.SemaphoreType.DMA((2 * OVER_Y,)),
        ],
        out_shape=[
            pltpu.HBM((8 * BLK, BLK), jnp.bfloat16),
            pltpu.HBM((2 * OVER_Y, HALF, BLK), jnp.bfloat16),
        ],
        compiler_params=params(24),
        cost_estimate=pl.CostEstimate(
            flops=2 * BLK * BLK * BLK * 8, bytes_accessed=13 << 20, transcendentals=0
        ),
        name="other_dot",
    )(rotated, own, near, last, far, far_last)


def mix_kernel(parts, copies, x_ref, out_ref):
    x = x_ref[...].astype(jnp.float32)
    rows = x.shape[0] // parts
    total = x[:rows]
    for part in range(1, parts):
        total = total + x[part * rows : (part + 1) * rows]
    tokens = rows // 16
    blocks = [
        [total[s * tokens : (s + 1) * tokens, c * HEAD_DIM : (c + 1) * HEAD_DIM] for c in range(4)]
        for s in range(16)
    ]
    flat = [blocks[s][c] for s in range(16) for c in range(4)]
    step = 1
    while step < 64:
        flat = [
            flat[i] + flat[i + step] if not i & step else flat[i - step] - flat[i]
            for i in range(64)
        ]
        step *= 2
    for s in range(16):
        for c in range(4):
            mixed = (flat[s * 4 + c] * (1.0 / math.sqrt(HEADS))).astype(jnp.bfloat16)
            for copy in range(copies):
                first = copy * rows + s * tokens
                out_ref[first : first + tokens, c * HEAD_DIM : (c + 1) * HEAD_DIM] = mixed


def mix(x, parts, copies):
    return pl.pallas_call(
        functools.partial(mix_kernel, parts, copies),
        out_shape=jax.ShapeDtypeStruct((x.shape[0] // parts * copies, x.shape[1]), jnp.bfloat16),
        compiler_params=params(16),
        name="mix",
    )(x)


def body(queries, keys, values, out_grad, o_weight, exponents, valid_lengths):
    scale = jnp.exp2(exponents.astype(jnp.float32))

    weights = lax.all_gather(o_weight, "z", axis=0, tiled=True)

    across = [(h * 2 + l, (1 - h) * 2 + 1 - l) for h in range(2) for l in range(2)]
    swap, pairs = [(0, 1), (1, 0)], [(0, 1), (1, 0), (2, 3), (3, 2)]

    picked = pick_units(out_grad)
    near = lax.ppermute(picked, ("xh", "xl"), across)

    queries, _ = lax.optimization_barrier((queries, picked))
    attended, probs = attention_fwd(valid_lengths, queries, keys, values)
    turned = lax.all_to_all(attended, TENSOR, 0, 0, tiled=True)
    rotated = lax.all_to_all(mix(turned, 1, 1), TENSOR, 0, 0, tiled=True)
    rotated_other = lax.ppermute(rotated, "xh", swap)
    near, rotated = lax.optimization_barrier((near, rotated))
    last = lax.ppermute(near[:OVER_Y], "y", pairs)
    far = lax.ppermute(near, "co", swap)
    own = own_dot(rotated, out_grad)
    last, far, own = lax.optimization_barrier((last, far, own))
    far_last = lax.ppermute(last, "co", swap)
    partial, kept = other_dot(rotated_other, own, near, last, far, far_last)
    summed = lax.psum_scatter(partial, "z", scatter_dimension=0, tiled=True)

    grad_rotated = grad_dot(out_grad, near, far, kept, weights, scale[None, :])
    turned = lax.all_to_all(grad_rotated.reshape(2 * BLK, BLK), ("xh",) + TENSOR, 0, 0, tiled=True)
    grad_attended = lax.all_to_all(mix(turned, 2, 1), TENSOR, 0, 0, tiled=True)
    grad_query, grad_key, grad_value = attention_bwd(probs, queries, keys, values, grad_attended)

    grad_weight = summed.astype(jnp.float32) * scale[:, None]
    return grad_query, grad_key, grad_value, grad_weight


def solution(mesh):
    fine = Mesh(mesh.devices.reshape(8, 2, 4, 2, 2), DP + TENSOR)
    return jax.shard_map(
        body,
        mesh=fine,
        in_specs=(
            P(DP, TENSOR),
            P(DP, TENSOR),
            P(DP, TENSOR),
            P(DP, None),
            P(TENSOR, DP),
            P(TENSOR),
            P(DP),
        ),
        out_specs=(P(DP, TENSOR), P(DP, TENSOR), P(DP, TENSOR), P(TENSOR, DP)),
        check_vma=False,
    )
```

```python
import functools
import math

import jax
import jax.numpy as jnp
from jax import lax
from jax.experimental import pallas as pl
from jax.experimental.pallas import tpu as pltpu
from jax.sharding import Mesh
from jax.sharding import PartitionSpec as P

HEADS = 64
HEAD_DIM = 128
DP = ("z", "xh")
TENSOR = ("y", "xl", "co")
BLK = 512


ANY = pl.BlockSpec(memory_space=pl.ANY)
HBM = pl.BlockSpec(memory_space=pltpu.HBM)
SMEM = pl.BlockSpec(memory_space=pltpu.SMEM)
VMEM = pl.BlockSpec(memory_space=pltpu.VMEM)
FWD, BWD = 18, 18
OVER_X = 6
BLOCKS = jax.ShapeDtypeStruct((8, BLK, BLK), jnp.bfloat16)
OVER_Y = 8 - OVER_X


def params(mib=60):
    return pltpu.CompilerParams(vmem_limit_bytes=mib * 1024 * 1024)


def dot(a, b, ca, cb):
    return lax.dot_general(a, b, (((ca,), (cb,)), ((), ())), preferred_element_type=jnp.float32)


HALF = BLK // 2


def fwd_kernel(len_ref, q_ref, k_ref, v_ref, att_ref, p_ref):
    for head in range(p_ref.shape[0]):
        cols = slice(head * HEAD_DIM, (head + 1) * HEAD_DIM)
        for first, keys in ((0, HALF), (HALF, BLK)):
            rows = slice(first, first + HALF)
            scores = dot(q_ref[rows, cols], k_ref[:keys, cols], 1, 1) * (1.0 / math.sqrt(HEAD_DIM))
            t = first + lax.broadcasted_iota(jnp.int32, scores.shape, 0)
            s = lax.broadcasted_iota(jnp.int32, scores.shape, 1)
            scores = jnp.where(s < jnp.minimum(t + 1, len_ref[0]), scores, -1e30)
            top = jnp.max(scores, axis=-1, keepdims=True)
            weights = jnp.exp(scores - top)
            probs = (weights * (1.0 / jnp.sum(weights, axis=-1, keepdims=True))).astype(jnp.bfloat16)
            p_ref[head, rows, :keys] = probs
            att_ref[rows, cols] = dot(probs, v_ref[:keys, cols], 1, 0).astype(jnp.bfloat16)


def attention_fwd(length, q, k, v):
    heads = q.shape[1] // HEAD_DIM
    return pl.pallas_call(
        fwd_kernel,
        in_specs=[SMEM, VMEM, VMEM, VMEM],
        out_specs=[VMEM, VMEM],
        out_shape=[
            jax.ShapeDtypeStruct(q.shape, jnp.bfloat16),
            jax.ShapeDtypeStruct((heads, BLK, BLK), jnp.bfloat16),
        ],
        compiler_params=params(FWD),
        cost_estimate=pl.CostEstimate(
            flops=heads * 4 * BLK * BLK * HEAD_DIM, bytes_accessed=6 << 20, transcendentals=heads * BLK * BLK
        ),
        name="attention_fwd",
    )(length, q, k, v)


def bwd_kernel(p_ref, q_ref, k_ref, v_ref, g_ref, dq_ref, dk_ref, dv_ref):
    for head in range(p_ref.shape[0]):
        cols = slice(head * HEAD_DIM, (head + 1) * HEAD_DIM)
        grad_keys, grad_values = [], []
        for first, keys in ((0, HALF), (HALF, BLK)):
            rows = slice(first, first + HALF)
            probs, grad = p_ref[head, rows, :keys], g_ref[rows, cols]
            grad_values.append(dot(probs, grad, 0, 0))
            grad_probs = dot(grad, v_ref[:keys, cols], 1, 1)
            wide = probs.astype(jnp.float32)
            centre = jnp.sum(wide * grad_probs, axis=-1, keepdims=True)
            grad_scores = (wide * (grad_probs - centre) * (1.0 / math.sqrt(HEAD_DIM))).astype(jnp.bfloat16)
            dq_ref[rows, cols] = dot(grad_scores, k_ref[:keys, cols], 1, 0).astype(jnp.bfloat16)
            grad_keys.append(dot(grad_scores, q_ref[rows, cols], 0, 0))
        for ref, (early, late) in ((dk_ref, grad_keys), (dv_ref, grad_values)):
            ref[:HALF, cols] = (early + late[:HALF]).astype(jnp.bfloat16)
            ref[HALF:, cols] = late[HALF:].astype(jnp.bfloat16)


def attention_bwd(probs, q, k, v, grad):
    heads = q.shape[1] // HEAD_DIM
    return pl.pallas_call(
        bwd_kernel,
        in_specs=[VMEM] * 5,
        out_specs=[VMEM] * 3,
        out_shape=[jax.ShapeDtypeStruct(q.shape, jnp.bfloat16)] * 3,
        compiler_params=params(BWD),
        cost_estimate=pl.CostEstimate(
            flops=heads * 8 * BLK * BLK * HEAD_DIM, bytes_accessed=6 << 20, transcendentals=0
        ),
        name="attention_bwd",
    )(probs, q, k, v, grad)


def unit_of(v, y_bit):
    return jnp.where(y_bit == 0, v, 7 - v)


def block_of(i, p):
    return 4 * jnp.where(i < 4, p[1], 1 - p[1]) + lax.rem(i, 4)


def place_here():
    return lax.axis_index("xh"), lax.axis_index("co"), lax.rem(lax.axis_index("y"), 2)


def piece_copies(refs, buf, sems, place):
    def target(group, v):
        unit = unit_of(v, place[2])
        rows = pl.ds(pl.multiple_of(lax.rem(unit, 2) * HALF, HALF), HALF)
        return buf.at[4 * group + unit // 2, rows]

    def start(group):
        over_x, over_y = refs[2 * group], refs[2 * group + 1]

        def begin(v):
            pltpu.make_async_copy(over_x.at[v], target(group, v), sems.at[8 * group + v]).start()

        each(0, OVER_X, begin)
        for w in range(OVER_Y):
            pltpu.make_async_copy(over_y.at[w], target(group, 7 - w), sems.at[8 * group + 7 - w]).start()

    def wait(i):
        group = i // 4
        for half in range(2):
            v = unit_of(2 * lax.rem(i, 4) + half, place[2])
            there = target(group, v)
            pltpu.make_async_copy(there, there, sems.at[8 * group + v]).wait()

    return start, wait, target


def each(first, count, step):
    def body(i, carry):
        step(i)
        return carry

    lax.fori_loop(first, first + count, body, 0)


def pick_kernel(grad_ref, out_ref, sems):
    x_hi, core, y_bit = place_here()

    def copy(v):
        unit = unit_of(v, y_bit)
        rows = pl.ds(pl.multiple_of(lax.rem(unit, 2) * HALF, HALF), HALF)
        column = pl.multiple_of((2 * (4 * core + unit // 2) + 1 - x_hi) * BLK, BLK)
        return pltpu.make_async_copy(grad_ref.at[rows, pl.ds(column, BLK)], out_ref.at[v], sems.at[v])

    each(0, OVER_X, lambda v: copy(v).start())
    each(0, OVER_X, lambda v: copy(v).wait())


def pick_units(out_grad):
    return pl.pallas_call(
        pick_kernel,
        in_specs=[HBM],
        out_specs=VMEM,
        scratch_shapes=[pltpu.SemaphoreType.DMA((OVER_X,))],
        out_shape=jax.ShapeDtypeStruct((OVER_X, HALF, BLK), jnp.bfloat16),
        compiler_params=params(60),
        name="pick_units",
    )(out_grad)


def take_kernel(grad_ref, out_ref, sems):
    x_hi, _, _ = place_here()

    def copy(z):
        column = pl.multiple_of((2 * z + x_hi) * BLK, BLK)
        return pltpu.make_async_copy(grad_ref.at[:, pl.ds(column, BLK)], out_ref.at[z], sems.at[z])

    each(0, 8, lambda z: copy(z).start())
    each(0, 8, lambda z: copy(z).wait())


def take_own(out_grad):
    return pl.pallas_call(
        take_kernel,
        in_specs=[HBM],
        out_specs=VMEM,
        scratch_shapes=[pltpu.SemaphoreType.DMA((8,))],
        out_shape=BLOCKS,
        compiler_params=params(18),
        cost_estimate=pl.CostEstimate(flops=0, bytes_accessed=8 << 20, transcendentals=0),
        name="take_own",
    )(out_grad)


def z_at(offset):
    return lax.rem(lax.axis_index("z") + offset, 8)


def at_z(z, core):
    return 4 * jnp.where(z // 4 == core, 0, 1) + lax.rem(z, 4)


def grad_kernel(own_ref, pieces_ref, scale_ref, *refs):
    w_refs, (out_ref, acc_ref) = refs[:9], refs[9:]
    x_hi, core, _ = place_here()
    scale = scale_ref[...]
    for r, offset in enumerate((0, 7, 1, 6, 2, 5, 3, 4)):
        z = z_at(offset)
        w = w_refs[r][...] if r < 7 else jnp.concatenate([w_refs[7][...], w_refs[8][...]])
        mine = dot(own_ref[z], w, 1, 1)
        theirs = dot(pieces_ref[at_z(z, core)], w, 1, 1)
        if r == 0:
            acc_ref[0], acc_ref[1] = mine, theirs
        elif r < 7:
            acc_ref[0] += mine
            acc_ref[1] += theirs
        else:
            out_ref[x_hi] = ((acc_ref[0] + mine) * scale).astype(jnp.bfloat16)
            out_ref[1 - x_hi] = ((acc_ref[1] + theirs) * scale).astype(jnp.bfloat16)


def grad_dot(own_blocks, pieces, weights, scale):
    return pl.pallas_call(
        grad_kernel,
        in_specs=[VMEM] * 12,
        out_specs=VMEM,
        scratch_shapes=[pltpu.VMEM((2, BLK, BLK), jnp.float32)],
        out_shape=jax.ShapeDtypeStruct((2, BLK, BLK), jnp.bfloat16),
        compiler_params=params(18),
        cost_estimate=pl.CostEstimate(
            flops=4 * BLK * BLK * BLK * 8, bytes_accessed=13 << 20, transcendentals=0
        ),
        name="grad_dot",
    )(own_blocks, pieces, scale, *weights)


def own_kernel(a_ref, own_ref, out_ref, at_ref):
    at_ref[...] = a_ref[...].T

    def step(offset):
        out_ref[offset] = dot(at_ref[...], own_ref[z_at(offset)], 1, 0).astype(jnp.bfloat16)

    each(0, 8, step)


def own_dot(rotated, own_blocks):
    return pl.pallas_call(
        own_kernel,
        in_specs=[VMEM, VMEM],
        out_specs=VMEM,
        scratch_shapes=[pltpu.VMEM((BLK, BLK), jnp.bfloat16)],
        out_shape=BLOCKS,
        compiler_params=params(18),
        cost_estimate=pl.CostEstimate(
            flops=2 * BLK * BLK * BLK * 8, bytes_accessed=9 << 20, transcendentals=0
        ),
        name="own_dot",
    )(rotated, own_blocks)


def other_kernel(a_ref, own_ref, near, last, far, far_last, *refs):
    out_refs, (pieces_ref, at_ref, sems) = refs[:9], refs[9:]
    place = place_here()
    start, wait, _ = piece_copies((near, last, far, far_last), pieces_ref, sems, place)
    start(0)
    start(1)
    at_ref[...] = a_ref[...].T
    each(0, 8, wait)
    for offset in (4, 3, 5, 2, 6, 1, 7, 0):
        block = pieces_ref[at_z(z_at(offset), place[1])]
        total = own_ref[offset].astype(jnp.float32) + dot(at_ref[...], block, 1, 0)
        total = total.astype(jnp.bfloat16)
        if offset == 4:
            out_refs[4][...], out_refs[8][...] = total[:HALF], total[HALF:]
        else:
            out_refs[offset][...] = total


def other_dot(rotated, own, near, last, far, far_last):
    block = jax.ShapeDtypeStruct((BLK, BLK), jnp.bfloat16)
    half = jax.ShapeDtypeStruct((HALF, BLK), jnp.bfloat16)
    *terms, pieces = pl.pallas_call(
        other_kernel,
        in_specs=[VMEM, VMEM, *[ANY] * 4],
        out_specs=[VMEM] * 10,
        scratch_shapes=[pltpu.VMEM((BLK, BLK), jnp.bfloat16), pltpu.SemaphoreType.DMA((16,))],
        out_shape=[half if offset in (4, 8) else block for offset in range(9)] + [BLOCKS],
        compiler_params=params(18),
        cost_estimate=pl.CostEstimate(
            flops=2 * BLK * BLK * BLK * 8, bytes_accessed=13 << 20, transcendentals=0
        ),
        name="other_dot",
    )(rotated, own, near, last, far, far_last)
    return terms, pieces


def mix_kernel(parts, copies, x_ref, out_ref):
    x = x_ref[...].astype(jnp.float32)
    rows = x.shape[0] // parts
    total = x[:rows]
    for part in range(1, parts):
        total = total + x[part * rows : (part + 1) * rows]
    tokens = rows // 16
    blocks = [
        [total[s * tokens : (s + 1) * tokens, c * HEAD_DIM : (c + 1) * HEAD_DIM] for c in range(4)]
        for s in range(16)
    ]
    flat = [blocks[s][c] for s in range(16) for c in range(4)]
    step = 1
    while step < 64:
        flat = [
            flat[i] + flat[i + step] if not i & step else flat[i - step] - flat[i]
            for i in range(64)
        ]
        step *= 2
    for s in range(16):
        for c in range(4):
            mixed = (flat[s * 4 + c] * (1.0 / math.sqrt(HEADS))).astype(jnp.bfloat16)
            for copy in range(copies):
                first = copy * rows + s * tokens
                out_ref[first : first + tokens, c * HEAD_DIM : (c + 1) * HEAD_DIM] = mixed


def mix(x, parts, copies):
    return pl.pallas_call(
        functools.partial(mix_kernel, parts, copies),
        out_shape=jax.ShapeDtypeStruct((x.shape[0] // parts * copies, x.shape[1]), jnp.bfloat16),
        compiler_params=params(16),
        name="mix",
    )(x)


def body(queries, keys, values, out_grad, o_weight, exponents, valid_lengths):
    scale = jnp.exp2(exponents.astype(jnp.float32))

    up, down = [(i, (i + 1) % 8) for i in range(8)], [((i + 1) % 8, i) for i in range(8)]

    def both(lower, upper, *after):
        lower, upper, *_ = lax.optimization_barrier((lower, upper, *after))
        return lax.ppermute(lower, "z", up), lax.ppermute(upper, "z", down)


    across = [(h * 2 + l, (1 - h) * 2 + 1 - l) for h in range(2) for l in range(2)]
    swap, pairs = [(0, 1), (1, 0)], [(0, 1), (1, 0), (2, 3), (3, 2)]

    picked = pick_units(out_grad)
    near = lax.ppermute(picked, ("xh", "xl"), across)

    queries, _ = lax.optimization_barrier((queries, picked))
    attended, probs = attention_fwd(valid_lengths, queries, keys, values)
    turned = lax.all_to_all(attended, TENSOR, 0, 0, tiled=True)
    ring = [both(o_weight, o_weight, attended)]
    own_blocks = take_own(lax.optimization_barrier((out_grad, attended))[0])
    mixed = mix(turned, 1, 1)
    ring.append(both(*ring[0], mixed))
    rotated = lax.all_to_all(mixed, TENSOR, 0, 0, tiled=True)
    rotated_other = lax.ppermute(rotated, "xh", swap)
    near, tied, *second = lax.optimization_barrier((near, rotated, *ring[1]))
    ring[1] = tuple(second)
    ring.append(both(*ring[1]))
    last = lax.ppermute(near[:OVER_Y], "y", pairs)
    far = lax.ppermute(near, "co", swap)
    own = own_dot(tied, own_blocks)
    last, far, own = lax.optimization_barrier((last, far, own))
    far_last = lax.ppermute(last, "co", swap)
    rotated_other, *third = lax.optimization_barrier((rotated_other, *ring[2]))
    ring[2] = tuple(third)
    ring.append(both(ring[2][0][:HALF], ring[2][1][HALF:]))
    terms, pieces = other_dot(rotated_other, own, near, last, far, far_last)
    weights = [o_weight, *ring[0], *ring[1], *ring[2], *ring[3]]
    grad_rotated = grad_dot(own_blocks, pieces, weights, scale[None, :])

    def add(first, second):
        return (first.astype(jnp.float32) + second.astype(jnp.float32)).astype(jnp.bfloat16)

    lower, upper = both(terms[4], terms[8])
    lower = jnp.concatenate([add(lower, terms[3][:HALF]), terms[3][HALF:]])
    upper = jnp.concatenate([terms[5][:HALF], add(upper, terms[5][HALF:])])
    lower, upper = both(lower, upper, grad_rotated)
    lower, upper = both(add(lower, terms[2]), add(upper, terms[6]))
    lower, upper = both(add(lower, terms[1]), add(upper, terms[7]))
    summed = lower.astype(jnp.float32) + upper.astype(jnp.float32) + terms[0].astype(jnp.float32)

    turned = lax.all_to_all(grad_rotated.reshape(2 * BLK, BLK), ("xh",) + TENSOR, 0, 0, tiled=True)
    grad_attended = lax.all_to_all(mix(turned, 2, 1), TENSOR, 0, 0, tiled=True)
    grad_query, grad_key, grad_value = attention_bwd(probs, queries, keys, values, grad_attended)

    grad_weight = summed * scale[:, None]
    return grad_query, grad_key, grad_value, grad_weight


def solution(mesh):
    fine = Mesh(mesh.devices.reshape(8, 2, 4, 2, 2), DP + TENSOR)
    return jax.shard_map(
        body,
        mesh=fine,
        in_specs=(
            P(DP, TENSOR),
            P(DP, TENSOR),
            P(DP, TENSOR),
            P(DP, None),
            P(TENSOR, DP),
            P(TENSOR),
            P(DP),
        ),
        out_specs=(P(DP, TENSOR), P(DP, TENSOR), P(DP, TENSOR), P(TENSOR, DP)),
        check_vma=False,
    )
```

```python
import functools
import math

import jax
import jax.numpy as jnp
from jax import lax
from jax.experimental import pallas as pl
from jax.experimental.pallas import tpu as pltpu
from jax.sharding import Mesh
from jax.sharding import PartitionSpec as P

HEADS = 64
HEAD_DIM = 128
DP = ("z", "xh")
TENSOR = ("y", "xl", "co")
BLK = 512


ANY = pl.BlockSpec(memory_space=pl.ANY)
HBM = pl.BlockSpec(memory_space=pltpu.HBM)
SMEM = pl.BlockSpec(memory_space=pltpu.SMEM)
VMEM = pl.BlockSpec(memory_space=pltpu.VMEM)
FWD, BWD = 18, 18
OVER_X = 6
BLOCKS = jax.ShapeDtypeStruct((8, BLK, BLK), jnp.bfloat16)
OVER_Y = 8 - OVER_X


def params(mib=60):
    return pltpu.CompilerParams(vmem_limit_bytes=mib * 1024 * 1024)


def dot(a, b, ca, cb):
    return lax.dot_general(a, b, (((ca,), (cb,)), ((), ())), preferred_element_type=jnp.float32)


HALF = BLK // 2


def fwd_kernel(len_ref, q_ref, k_ref, v_ref, att_ref, p_ref):
    for head in range(p_ref.shape[0]):
        cols = slice(head * HEAD_DIM, (head + 1) * HEAD_DIM)
        for first, keys in ((0, HALF), (HALF, BLK)):
            rows = slice(first, first + HALF)
            scores = dot(q_ref[rows, cols], k_ref[:keys, cols], 1, 1) * (1.0 / math.sqrt(HEAD_DIM))
            t = first + lax.broadcasted_iota(jnp.int32, scores.shape, 0)
            s = lax.broadcasted_iota(jnp.int32, scores.shape, 1)
            scores = jnp.where(s < jnp.minimum(t + 1, len_ref[0]), scores, -1e30)
            top = jnp.max(scores, axis=-1, keepdims=True)
            weights = jnp.exp(scores - top)
            probs = (weights * (1.0 / jnp.sum(weights, axis=-1, keepdims=True))).astype(jnp.bfloat16)
            p_ref[head, rows, :keys] = probs
            att_ref[rows, cols] = dot(probs, v_ref[:keys, cols], 1, 0).astype(jnp.bfloat16)


def attention_fwd(length, q, k, v):
    heads = q.shape[1] // HEAD_DIM
    return pl.pallas_call(
        fwd_kernel,
        in_specs=[SMEM, VMEM, VMEM, VMEM],
        out_specs=[VMEM, VMEM],
        out_shape=[
            jax.ShapeDtypeStruct(q.shape, jnp.bfloat16),
            jax.ShapeDtypeStruct((heads, BLK, BLK), jnp.bfloat16),
        ],
        compiler_params=params(FWD),
        cost_estimate=pl.CostEstimate(
            flops=heads * 4 * BLK * BLK * HEAD_DIM, bytes_accessed=6 << 20, transcendentals=heads * BLK * BLK
        ),
        name="attention_fwd",
    )(length, q, k, v)


def bwd_kernel(p_ref, q_ref, k_ref, v_ref, g_ref, dq_ref, dk_ref, dv_ref):
    for head in range(p_ref.shape[0]):
        cols = slice(head * HEAD_DIM, (head + 1) * HEAD_DIM)
        grad_keys, grad_values = [], []
        for first, keys in ((0, HALF), (HALF, BLK)):
            rows = slice(first, first + HALF)
            probs, grad = p_ref[head, rows, :keys], g_ref[rows, cols]
            grad_values.append(dot(probs, grad, 0, 0))
            grad_probs = dot(grad, v_ref[:keys, cols], 1, 1)
            wide = probs.astype(jnp.float32)
            centre = jnp.sum(wide * grad_probs, axis=-1, keepdims=True)
            grad_scores = (wide * (grad_probs - centre) * (1.0 / math.sqrt(HEAD_DIM))).astype(jnp.bfloat16)
            dq_ref[rows, cols] = dot(grad_scores, k_ref[:keys, cols], 1, 0).astype(jnp.bfloat16)
            grad_keys.append(dot(grad_scores, q_ref[rows, cols], 0, 0))
        for ref, (early, late) in ((dk_ref, grad_keys), (dv_ref, grad_values)):
            ref[:HALF, cols] = (early + late[:HALF]).astype(jnp.bfloat16)
            ref[HALF:, cols] = late[HALF:].astype(jnp.bfloat16)


def attention_bwd(probs, q, k, v, grad):
    heads = q.shape[1] // HEAD_DIM
    return pl.pallas_call(
        bwd_kernel,
        in_specs=[VMEM] * 5,
        out_specs=[VMEM] * 3,
        out_shape=[jax.ShapeDtypeStruct(q.shape, jnp.bfloat16)] * 3,
        compiler_params=params(BWD),
        cost_estimate=pl.CostEstimate(
            flops=heads * 8 * BLK * BLK * HEAD_DIM, bytes_accessed=6 << 20, transcendentals=0
        ),
        name="attention_bwd",
    )(probs, q, k, v, grad)


def unit_of(v, y_bit):
    return jnp.where(y_bit == 0, v, 6 - 2 * (v // 2) + lax.rem(v, 2))


def block_of(i, p):
    return 4 * jnp.where(i < 4, p[1], 1 - p[1]) + lax.rem(i, 4)


def place_here():
    return lax.axis_index("xh"), lax.axis_index("co"), lax.rem(lax.axis_index("y"), 2)


def piece_copies(refs, buf, sems, place):
    def target(group, v):
        unit = unit_of(v, place[2])
        rows = pl.ds(pl.multiple_of(lax.rem(unit, 2) * HALF, HALF), HALF)
        return buf.at[4 * group + unit // 2, rows]

    def start(group):
        over_x, over_y = refs[2 * group], refs[2 * group + 1]

        def begin(v):
            pltpu.make_async_copy(over_x.at[v], target(group, v), sems.at[8 * group + v]).start()

        each(0, OVER_X, begin)
        for w in range(OVER_Y):
            v = OVER_X + w
            pltpu.make_async_copy(over_y.at[w], target(group, v), sems.at[8 * group + v]).start()

    def wait(i):
        group = i // 4
        for half in range(2):
            v = unit_of(2 * lax.rem(i, 4) + half, place[2])
            there = target(group, v)
            pltpu.make_async_copy(there, there, sems.at[8 * group + v]).wait()

    return start, wait, target


def each(first, count, step):
    def body(i, carry):
        step(i)
        return carry

    lax.fori_loop(first, first + count, body, 0)


def pick_units(out_grad):
    x_hi, core, y_bit = place_here()

    def block(j):
        column = (2 * (4 * core + jnp.where(y_bit == 0, j, 3 - j)) + 1 - x_hi) * BLK
        return lax.dynamic_slice(out_grad, (0, column), (BLK, BLK))

    return jnp.stack([block(j) for j in range(OVER_X // 2)]).reshape(OVER_X, HALF, BLK)


def take_kernel(grad_ref, out_ref, sems):
    x_hi, _, _ = place_here()

    def copy(z):
        column = pl.multiple_of((2 * z + x_hi) * BLK, BLK)
        return pltpu.make_async_copy(grad_ref.at[:, pl.ds(column, BLK)], out_ref.at[z], sems.at[z])

    each(0, 8, lambda z: copy(z).start())
    each(0, 8, lambda z: copy(z).wait())


def take_own(out_grad):
    return pl.pallas_call(
        take_kernel,
        in_specs=[HBM],
        out_specs=VMEM,
        scratch_shapes=[pltpu.SemaphoreType.DMA((8,))],
        out_shape=BLOCKS,
        compiler_params=params(18),
        cost_estimate=pl.CostEstimate(flops=0, bytes_accessed=8 << 20, transcendentals=0),
        name="take_own",
    )(out_grad)


def z_at(offset):
    return lax.rem(lax.axis_index("z") + offset, 8)


def at_z(z, core):
    return 4 * jnp.where(z // 4 == core, 0, 1) + lax.rem(z, 4)


def grad_kernel(own_ref, pieces_ref, scale_ref, *refs):
    w_refs, (out_ref, acc_ref) = refs[:9], refs[9:]
    x_hi, core, _ = place_here()
    scale = scale_ref[...]
    for r, offset in enumerate((0, 7, 1, 6, 2, 5, 3, 4)):
        z = z_at(offset)
        w = w_refs[r][...] if r < 7 else jnp.concatenate([w_refs[7][...], w_refs[8][...]])
        mine = dot(own_ref[z], w, 1, 1)
        theirs = dot(pieces_ref[at_z(z, core)], w, 1, 1)
        if r == 0:
            acc_ref[0], acc_ref[1] = mine, theirs
        elif r < 7:
            acc_ref[0] += mine
            acc_ref[1] += theirs
        else:
            out_ref[x_hi] = ((acc_ref[0] + mine) * scale).astype(jnp.bfloat16)
            out_ref[1 - x_hi] = ((acc_ref[1] + theirs) * scale).astype(jnp.bfloat16)


def grad_dot(own_blocks, pieces, weights, scale):
    return pl.pallas_call(
        grad_kernel,
        in_specs=[VMEM] * 12,
        out_specs=VMEM,
        scratch_shapes=[pltpu.VMEM((2, BLK, BLK), jnp.float32)],
        out_shape=jax.ShapeDtypeStruct((2, BLK, BLK), jnp.bfloat16),
        compiler_params=params(18),
        cost_estimate=pl.CostEstimate(
            flops=4 * BLK * BLK * BLK * 8, bytes_accessed=13 << 20, transcendentals=0
        ),
        name="grad_dot",
    )(own_blocks, pieces, scale, *weights)


def own_kernel(a_ref, own_ref, out_ref, at_ref):
    at_ref[...] = a_ref[...].T

    def step(offset):
        out_ref[offset] = dot(at_ref[...], own_ref[z_at(offset)], 1, 0).astype(jnp.bfloat16)

    each(0, 8, step)


def own_dot(rotated, own_blocks):
    return pl.pallas_call(
        own_kernel,
        in_specs=[VMEM, VMEM],
        out_specs=VMEM,
        scratch_shapes=[pltpu.VMEM((BLK, BLK), jnp.bfloat16)],
        out_shape=BLOCKS,
        compiler_params=params(18),
        cost_estimate=pl.CostEstimate(
            flops=2 * BLK * BLK * BLK * 8, bytes_accessed=9 << 20, transcendentals=0
        ),
        name="own_dot",
    )(rotated, own_blocks)


def other_kernel(a_ref, own_ref, near, last, far, far_last, *refs):
    out_refs, (pieces_ref, at_ref, sems) = refs[:9], refs[9:]
    place = place_here()
    start, wait, _ = piece_copies((near, last, far, far_last), pieces_ref, sems, place)
    start(0)
    start(1)
    at_ref[...] = a_ref[...].T
    each(0, 8, wait)
    for offset in (4, 3, 5, 2, 6, 1, 7, 0):
        block = pieces_ref[at_z(z_at(offset), place[1])]
        total = own_ref[offset].astype(jnp.float32) + dot(at_ref[...], block, 1, 0)
        total = total.astype(jnp.bfloat16)
        if offset == 4:
            out_refs[4][...], out_refs[8][...] = total[:HALF], total[HALF:]
        else:
            out_refs[offset][...] = total


def other_dot(rotated, own, near, last, far, far_last):
    block = jax.ShapeDtypeStruct((BLK, BLK), jnp.bfloat16)
    half = jax.ShapeDtypeStruct((HALF, BLK), jnp.bfloat16)
    *terms, pieces = pl.pallas_call(
        other_kernel,
        in_specs=[VMEM, VMEM, *[ANY] * 4],
        out_specs=[VMEM] * 10,
        scratch_shapes=[pltpu.VMEM((BLK, BLK), jnp.bfloat16), pltpu.SemaphoreType.DMA((16,))],
        out_shape=[half if offset in (4, 8) else block for offset in range(9)] + [BLOCKS],
        compiler_params=params(18),
        cost_estimate=pl.CostEstimate(
            flops=2 * BLK * BLK * BLK * 8, bytes_accessed=13 << 20, transcendentals=0
        ),
        name="other_dot",
    )(rotated, own, near, last, far, far_last)
    return terms, pieces


def mix_kernel(parts, copies, x_ref, out_ref):
    x = x_ref[...].astype(jnp.float32)
    rows = x.shape[0] // parts
    total = x[:rows]
    for part in range(1, parts):
        total = total + x[part * rows : (part + 1) * rows]
    tokens = rows // 16
    blocks = [
        [total[s * tokens : (s + 1) * tokens, c * HEAD_DIM : (c + 1) * HEAD_DIM] for c in range(4)]
        for s in range(16)
    ]
    flat = [blocks[s][c] for s in range(16) for c in range(4)]
    step = 1
    while step < 64:
        flat = [
            flat[i] + flat[i + step] if not i & step else flat[i - step] - flat[i]
            for i in range(64)
        ]
        step *= 2
    for s in range(16):
        for c in range(4):
            mixed = (flat[s * 4 + c] * (1.0 / math.sqrt(HEADS))).astype(jnp.bfloat16)
            for copy in range(copies):
                first = copy * rows + s * tokens
                out_ref[first : first + tokens, c * HEAD_DIM : (c + 1) * HEAD_DIM] = mixed


def mix(x, parts, copies):
    return pl.pallas_call(
        functools.partial(mix_kernel, parts, copies),
        out_shape=jax.ShapeDtypeStruct((x.shape[0] // parts * copies, x.shape[1]), jnp.bfloat16),
        compiler_params=params(16),
        name="mix",
    )(x)


def body(queries, keys, values, out_grad, o_weight, exponents, valid_lengths):
    scale = jnp.exp2(exponents.astype(jnp.float32))

    up, down = [(i, (i + 1) % 8) for i in range(8)], [((i + 1) % 8, i) for i in range(8)]

    def both(lower, upper, *after):
        lower, upper, *_ = lax.optimization_barrier((lower, upper, *after))
        return lax.ppermute(lower, "z", up), lax.ppermute(upper, "z", down)


    across = [(h * 2 + l, (1 - h) * 2 + 1 - l) for h in range(2) for l in range(2)]
    swap, pairs = [(0, 1), (1, 0)], [(0, 1), (1, 0), (2, 3), (3, 2)]

    picked = pick_units(out_grad)
    near = lax.ppermute(picked, ("xh", "xl"), across)

    queries, _ = lax.optimization_barrier((queries, picked))
    attended, probs = attention_fwd(valid_lengths, queries, keys, values)
    turned = lax.all_to_all(attended, TENSOR, 0, 0, tiled=True)
    ring = [both(o_weight, o_weight, attended)]
    own_blocks = take_own(lax.optimization_barrier((out_grad, attended))[0])
    mixed = mix(turned, 1, 1)
    ring.append(both(*ring[0], mixed))
    rotated = lax.all_to_all(mixed, TENSOR, 0, 0, tiled=True)
    rotated_other = lax.ppermute(rotated, "xh", swap)
    near, tied, *second = lax.optimization_barrier((near, rotated, *ring[1]))
    ring[1] = tuple(second)
    ring.append(both(*ring[1]))
    last = lax.ppermute(near[:OVER_Y], "y", pairs)
    far = lax.ppermute(near, "co", swap)
    own = own_dot(tied, own_blocks)
    last, far, own = lax.optimization_barrier((last, far, own))
    far_last = lax.ppermute(last, "co", swap)
    rotated_other, *third = lax.optimization_barrier((rotated_other, *ring[2]))
    ring[2] = tuple(third)
    ring.append(both(ring[2][0][:HALF], ring[2][1][HALF:]))
    terms, pieces = other_dot(rotated_other, own, near, last, far, far_last)
    weights = [o_weight, *ring[0], *ring[1], *ring[2], *ring[3]]
    grad_rotated = grad_dot(own_blocks, pieces, weights, scale[None, :])

    def add(first, second):
        return (first.astype(jnp.float32) + second.astype(jnp.float32)).astype(jnp.bfloat16)

    lower, upper = both(terms[4], terms[8])
    lower = jnp.concatenate([add(lower, terms[3][:HALF]), terms[3][HALF:]])
    upper = jnp.concatenate([terms[5][:HALF], add(upper, terms[5][HALF:])])
    lower, upper = both(lower, upper, grad_rotated)
    lower, upper = both(add(lower, terms[2]), add(upper, terms[6]))
    lower, upper = both(add(lower, terms[1]), add(upper, terms[7]))
    summed = lower.astype(jnp.float32) + upper.astype(jnp.float32) + terms[0].astype(jnp.float32)

    turned = lax.all_to_all(grad_rotated.reshape(2 * BLK, BLK), ("xh",) + TENSOR, 0, 0, tiled=True)
    grad_attended = lax.all_to_all(mix(turned, 2, 1), TENSOR, 0, 0, tiled=True)
    grad_query, grad_key, grad_value = attention_bwd(probs, queries, keys, values, grad_attended)

    grad_weight = summed * scale[:, None]
    return grad_query, grad_key, grad_value, grad_weight


def solution(mesh):
    fine = Mesh(mesh.devices.reshape(8, 2, 4, 2, 2), DP + TENSOR)
    return jax.shard_map(
        body,
        mesh=fine,
        in_specs=(
            P(DP, TENSOR),
            P(DP, TENSOR),
            P(DP, TENSOR),
            P(DP, None),
            P(TENSOR, DP),
            P(TENSOR),
            P(DP),
        ),
        out_specs=(P(DP, TENSOR), P(DP, TENSOR), P(DP, TENSOR), P(TENSOR, DP)),
        check_vma=False,
    )
```
